32 devices in a mesh: groups: 2 (over y), left: 4 (over z), right: 2 (over x), mpo: 2 (over core).
Axes of the slice: x: 2, y: 2, z: 4, core: 2. Of those that a mesh axis runs over, the one named last changes fastest.
Arguments:
- theta: bfloat16 [16, 128, 128], P(('groups', 'left', 'right')), parts along dimension 0, may hold values from -6 to 6
- left_env: bfloat16 [8, 64, 128, 128], P(('groups', 'mpo'), 'left'), parts along dimension 0, may hold values from -1 to 1
- right_env: bfloat16 [8, 32, 128, 128], P(('groups', 'mpo'), 'right'), parts along dimension 0, may hold values from -1 to 1
- terms: int32 [8, 2, 2, 16, 14], P(('groups', 'left'), 'right', 'mpo'), parts along dimension 0, may hold values from 0 to 31, as said below
Outputs:
- h_theta: float32 [16, 128, 128], P(('groups', 'left', 'right')), parts along dimension 0
- h_second: float32 [16, 128, 128], P(('groups', 'left', 'right')), parts along dimension 0
The draws below stay inside these ranges and needn't reach their ends.
There are 2 independent parts, one for each index of `groups`. The reference program is written for one: setup_inputs(seed, part) draws one part's arguments, and reference() takes and returns one part's arrays. A program takes and returns all parts, laid end to end along the dimension named above; each array names one. Nothing has to cross between parts.
Inputs may be any that keep to these rules, and one draw needn't show every extreme that they name: `terms`: field 0 is below 32, field 1 below 2, the 6 right tiles below 16, the 6 output left indices below 4. In the list of every device, at most 8 entries name one target right index, and some target is named by exactly 8 entries.
All inputs are finite; a program needn't handle non-finite values.
Results may differ from the reference program's by a relative error of at most 0.0016.
Values may be sent and summed in bfloat16 or wider, within the bound.
No kernel may reach another device: no remote copies, remote signals or barrier semaphores. Data moves between devices by JAX's collectives and lax.ppermute only.
A program may use at most 64 MiB of HBM per device.

```python
import jax
import jax.numpy as jnp
from jax import lax

TILE = 128
W = 4
LT_DEV = 16
RT_DEV = 16
PA = 16
RB = 6
W_DEV = 2
NTH = 8
NLT = 64
NRT = 32
N_LEFT = 4
N_RIGHT = 2
N_MPO = 2


def draw_terms(key, part):
    key = jax.random.fold_in(key, 11)
    subkeys = jax.random.split(key, 6)
    lead = (N_LEFT, N_RIGHT, N_MPO)
    left_local = jax.random.randint(subkeys[0], lead + (PA,), 0, W // N_MPO * LT_DEV)
    main_peer = jax.random.randint(subkeys[1], lead + (1,), 0, N_RIGHT)
    other_peer = (main_peer + 1 + jax.random.randint(subkeys[2], lead + (PA,), 0, N_RIGHT - 1)) % N_RIGHT
    position = jnp.arange(PA, dtype=jnp.int32)
    sorted_peer = jnp.where(position < PA // 2, main_peer, other_peer)
    scores = jax.random.randint(subkeys[3], lead + (PA,), 0, 1 << 20) * PA + position
    shuffle = jnp.argsort(scores, axis=-1, stable=True)
    target_right = jnp.take_along_axis(sorted_peer, shuffle, axis=-1)
    right_local = jax.random.randint(subkeys[4], lead + (PA, RB), 0, RT_DEV)
    out_left = jax.random.randint(subkeys[5], lead + (PA, RB), 0, N_LEFT)
    return jnp.concatenate([left_local[..., None], target_right[..., None], right_local, out_left], axis=-1).astype(jnp.int32)


def draw_theta(key, part):
    key = jax.random.fold_in(key, 31)
    key_common, key_noise = jax.random.split(key)
    common = jax.random.normal(key_common, (TILE, TILE), jnp.float32)
    noise = jax.random.normal(key_noise, (NTH, TILE, TILE), jnp.float32)
    share = 0.6
    values = share * common[None] + (1.0 - share * share) ** 0.5 * noise
    return jnp.clip(values, -6.0, 6.0).astype(jnp.bfloat16)


def draw_left_env(key, part):
    key = jax.random.fold_in(key, 41)
    key_common, key_noise = jax.random.split(key)
    common = jax.random.normal(key_common, (TILE, TILE), jnp.float32)
    noise = jax.random.normal(key_noise, (W, NLT, TILE, TILE), jnp.float32)
    share = 0.6
    values = share * common[None, None] + (1.0 - share * share) ** 0.5 * noise
    return (jnp.clip(values, -4.0, 4.0) * TILE ** (-0.5)).astype(jnp.bfloat16)


def draw_right_env(key, part):
    key = jax.random.fold_in(key, 51)
    key_common, key_noise = jax.random.split(key)
    common = jax.random.normal(key_common, (TILE, TILE), jnp.float32)
    noise = jax.random.normal(key_noise, (W, NRT, TILE, TILE), jnp.float32)
    share = 0.6
    per_tile = N_MPO * PA * RB
    spread = (TILE * (per_tile + share ** 6 * per_tile * per_tile)) ** (-0.5)
    values = share * common[None, None] + (1.0 - share * share) ** 0.5 * noise
    return (jnp.clip(values, -4.0, 4.0) * spread).astype(jnp.bfloat16)


def setup_inputs(seed: int = 0, part: int = 0) -> dict:
    seeds = jax.random.split(jax.random.key(seed), 5)
    own_keys = jax.random.split(jax.random.fold_in(seeds[4], part), 5)
    return {
        "theta": draw_theta(jax.random.fold_in(jax.random.fold_in(seeds[4], part), 71), part),
        "left_env": draw_left_env(jax.random.fold_in(jax.random.fold_in(seeds[4], part), 71), part),
        "right_env": draw_right_env(jax.random.fold_in(jax.random.fold_in(seeds[4], part), 71), part),
        "terms": draw_terms(jax.random.fold_in(jax.random.fold_in(seeds[4], part), 71), part),
    }


def apply_ham(vector, left_env, right_env, terms):

    def per_device(accum, device_index):
        left_id = device_index // (N_RIGHT * N_MPO)
        right_id = device_index // N_MPO % N_RIGHT
        mpo_id = device_index % N_MPO
        entries = terms[left_id, right_id, mpo_id]
        left_local = entries[:, 0]
        target_right = entries[:, 1]
        right_local = entries[:, 2:2 + RB]
        out_left = entries[:, 2 + RB:]
        mpo_index = mpo_id * W_DEV + left_local // LT_DEV
        left_pick = left_env[mpo_index, left_id * LT_DEV + left_local % LT_DEV]
        source = vector[left_id * N_RIGHT + right_id]
        inter = jnp.einsum('sik,kj->sij', left_pick.astype(jnp.float32), source.astype(jnp.float32)).astype(jnp.bfloat16)
        right_pick = right_env[mpo_index[:, None], target_right[:, None] * RT_DEV + right_local]
        products = jnp.einsum('sij,srjk->srik', inter.astype(jnp.float32), right_pick.astype(jnp.float32))
        target = (out_left * N_RIGHT + target_right[:, None]).reshape(-1)
        accum = accum.at[target].add(products.reshape(-1, TILE, TILE))
        return (accum, None)
    start = jnp.zeros((NTH, TILE, TILE), jnp.float32)
    return lax.scan(per_device, start, jnp.arange(N_LEFT * N_RIGHT * N_MPO, dtype=jnp.int32))[0]

def reference(theta, left_env, right_env, terms):
    h_theta = apply_ham(theta, left_env, right_env, terms)
    norm_scale = jnp.sqrt(jnp.mean(h_theta * h_theta) + 1e-06)
    second = (h_theta / norm_scale).astype(jnp.bfloat16)
    h_second = apply_ham(second, left_env, right_env, terms)
    return (h_theta, h_second)
```

```python
import functools

import jax
import jax.numpy as jnp
from jax import lax
from jax.experimental import pallas as pl
from jax.experimental.pallas import tpu as pltpu
from jax.sharding import PartitionSpec as P

CAP = 8
VMEM = pl.BlockSpec(memory_space=pltpu.VMEM)
SMEM = pl.BlockSpec(memory_space=pltpu.SMEM)


def apply_entries(lists, vecs, left_ref, right_ref, acc, sel, rt_dev, lt_dev):
    me_left = lax.axis_index("left")
    me_right = lax.axis_index("right")
    rows, fields = lists[0].shape
    per = (fields - 2) // 2
    exact = CAP * len(lists) == rows
    acc[...] = jnp.zeros_like(acc)
    counts = []
    for q, terms in enumerate(lists):
        count = jnp.int32(0)
        for e in range(rows):
            sel[q, count] = jnp.int32(e)
            count = count + (terms[e, 1] == me_right).astype(jnp.int32)
        counts.append(count)

    def entry(q, n):
        terms = lists[q]
        e = sel[q, n]
        k = terms[e, 0]
        inter = jnp.dot(
            left_ref[k], vecs[q], preferred_element_type=jnp.float32
        ).astype(jnp.bfloat16)
        base = (k // lt_dev) * rt_dev
        for j in range(0, per, 2):
            pair = jnp.concatenate(
                [right_ref[base + terms[e, 2 + j]], right_ref[base + terms[e, 3 + j]]], axis=1
            )
            product = jnp.dot(inter, pair, preferred_element_type=jnp.float32)
            tile = product.shape[1] // 2
            for i in range(2):
                o = terms[e, 2 + per + j + i] ^ me_left
                acc[o] += product[:, i * tile:(i + 1) * tile]

    for q in range(len(lists)):
        if exact:
            for n in range(CAP):
                entry(q, n)
        else:
            pl.loop(0, counts[q])(functools.partial(entry, q))


def first_kernel(nr, nl, rt_dev, lt_dev, *refs):
    lists = refs[:nr]
    thetas = refs[nr:2 * nr]
    left_ref, right_ref = refs[2 * nr:2 * nr + 2]
    outs = refs[2 * nr + 2:2 * nr + 2 + nl]
    acc, sel = refs[2 * nr + 2 + nl:]
    vecs = [t[0] for t in thetas]
    apply_entries(lists, vecs, left_ref, right_ref, acc, sel, rt_dev, lt_dev)
    for s in range(nl):
        outs[s][...] = acc[s]


def second_kernel(nr, nl, rt_dev, lt_dev, count, *refs):
    lists = refs[:nr]
    tiles = refs[nr:2 * nr]
    sums = refs[2 * nr]
    left_ref, right_ref = refs[2 * nr + 1:2 * nr + 3]
    outs = refs[2 * nr + 3:2 * nr + 3 + nl]
    acc, sel = refs[2 * nr + 3 + nl:]
    square_sum = jnp.sum(sums[...], keepdims=True)
    scale = jnp.sqrt(square_sum / count + 1e-06)
    vecs = [(t[...] / scale).astype(jnp.bfloat16) for t in tiles]
    apply_entries(lists, vecs, left_ref, right_ref, acc, sel, rt_dev, lt_dev)
    for s in range(nl):
        outs[s][...] = acc[s]


def squares_kernel(*refs):
    out = refs[-1]
    total = None
    for ref in refs[:-1]:
        rows, tile = ref.shape
        square = ref[...] * ref[...]
        part = jnp.sum(square.reshape(rows // 8, 8, tile), axis=0)
        total = part if total is None else total + part
    out[...] = total


def swap(value, axis, offset):
    size = lax.axis_size(axis)
    return lax.ppermute(value, axis, [(i, i ^ offset) for i in range(size)])


def local(theta, left_env, right_env, terms):
    tile = theta.shape[-1]
    lt_dev = left_env.shape[1]
    rt_dev = right_env.shape[1]
    left_flat = left_env.reshape(-1, tile, tile)
    right_flat = right_env.reshape(-1, tile, tile)
    nl = lax.axis_size("left")
    nr = lax.axis_size("right")
    entries = terms[0, 0, 0]
    lists = [entries] + [swap(entries, "right", s) for s in range(1, nr)]
    thetas = [theta] + [swap(theta, "right", s) for s in range(1, nr)]
    flat = jax.ShapeDtypeStruct((tile, tile), jnp.float32)
    scratch = [pltpu.VMEM((nl, tile, tile), jnp.float32), pltpu.SMEM((nr, entries.shape[0] + 1), jnp.int32)]
    params = pltpu.CompilerParams(vmem_limit_bytes=32 << 20)

    def reduce_tiles(parts):
        own = parts[0]
        for s in range(1, nl):
            own = own + swap(parts[s], "left", s)
        return own + lax.ppermute(own, "mpo", [(0, 1), (1, 0)])

    parts = pl.pallas_call(
        functools.partial(first_kernel, nr, nl, rt_dev, lt_dev),
        out_shape=[flat] * nl,
        in_specs=[SMEM] * nr + [VMEM] * (nr + 2),
        out_specs=[VMEM] * nl,
        scratch_shapes=scratch,
        compiler_params=params,
        name="first_product",
    )(*lists, *thetas, left_flat, right_flat)
    h_theta = reduce_tiles(parts)

    tiles = [h_theta] + [swap(h_theta, "right", s) for s in range(1, nr)]
    squares = pl.pallas_call(
        squares_kernel,
        out_shape=jax.ShapeDtypeStruct((8, tile), jnp.float32),
        in_specs=[VMEM] * nr,
        out_specs=VMEM,
        name="squares",
    )(*tiles)
    sums = squares
    for s in range(1, nl):
        sums = sums + swap(squares, "left", s)

    parts = pl.pallas_call(
        functools.partial(second_kernel, nr, nl, rt_dev, lt_dev, nl * nr * tile * tile),
        out_shape=[flat] * nl,
        in_specs=[SMEM] * nr + [VMEM] * (nr + 3),
        out_specs=[VMEM] * nl,
        scratch_shapes=scratch,
        compiler_params=params,
        name="second_product",
    )(*lists, *tiles, sums, left_flat, right_flat)
    h_second = reduce_tiles(parts)
    return h_theta[None], h_second[None]


def solution(mesh):
    in_specs = (
        P(("groups", "left", "right"), None, None),
        P(("groups", "mpo"), "left", None, None),
        P(("groups", "mpo"), "right", None, None),
        P(("groups", "left"), "right", "mpo", None, None),
    )
    out_specs = (
        P(("groups", "left", "right"), None, None),
        P(("groups", "left", "right"), None, None),
    )
    return jax.shard_map(local, mesh=mesh, in_specs=in_specs, out_specs=out_specs, check_vma=False)
```

```python
import functools

import jax
import jax.numpy as jnp
from jax import lax
from jax.experimental import pallas as pl
from jax.experimental.pallas import tpu as pltpu
from jax.sharding import PartitionSpec as P

CAP = 8
VMEM = pl.BlockSpec(memory_space=pltpu.VMEM)
HBM = pl.BlockSpec(memory_space=pltpu.HBM)
SMEM = pl.BlockSpec(memory_space=pltpu.SMEM)


def dot(a, b):
    return jnp.dot(a, b, preferred_element_type=jnp.float32)


def pick_entries(terms, sel):
    me_right = lax.axis_index("right")
    count = jnp.int32(0)
    for e in range(terms.shape[-1]):
        sel[count] = jnp.int32(e)
        count = count + (terms[1, 0, e] == me_right).astype(jnp.int32)
    return count


def apply_list(terms, sel, count, vec, left_ref, right_ref, acc, inter, dims):
    lt_dev, rt_dev, exact = dims
    me_left = lax.axis_index("left")
    fields, _, rows = terms.shape
    per = (fields - 2) // 2
    tile = vec.shape[-1]

    def spread(e, y):
        base = (terms[0, 0, e] // lt_dev) * rt_dev
        for j in range(per):
            product = dot(y, right_ref[base + terms[2 + j, 0, e]])
            acc[terms[2 + per + j, 0, e] ^ me_left] += product

    if exact:
        picks = jnp.concatenate([left_ref[terms[0, 0, sel[n]]] for n in range(CAP)], axis=0)
        inter[...] = dot(picks, vec).astype(jnp.bfloat16).reshape(CAP, tile, tile)
        for n in range(CAP):
            spread(sel[n], inter[n])
    else:

        def one(n):
            e = sel[n]
            spread(e, dot(left_ref[terms[0, 0, e]], vec).astype(jnp.bfloat16))

        pl.loop(0, count)(one)


def load_kernel(left_hbm, right_hbm, left_ref, right_ref, sems):
    copies = [
        pltpu.make_async_copy(left_hbm, left_ref, sems.at[0]),
        pltpu.make_async_copy(right_hbm, right_ref, sems.at[1]),
    ]
    for copy in copies:
        copy.start()
    for copy in copies:
        copy.wait()


def own_kernel(dims, terms, theta, left_ref, right_ref, out, sel, inter):
    out[...] = jnp.zeros_like(out)
    count = pick_entries(terms, sel)
    apply_list(terms, sel, count, theta[0], left_ref, right_ref, out, inter, dims)


def rest_kernel(dims, count, *refs):
    lists = refs[:count]
    thetas = refs[count:2 * count]
    left_ref, right_ref, start, out, sel, inter = refs[2 * count:]
    out[...] = start[...]
    for terms, theta in zip(lists, thetas):
        picked = pick_entries(terms, sel)
        apply_list(terms, sel, picked, theta[0], left_ref, right_ref, out, inter, dims)


def second_kernel(dims, nr, nl, chip_pair, elements, *refs):
    lists = refs[:nr]
    tiles = refs[nr:2 * nr]
    sums = refs[2 * nr:2 * nr + nl]
    left_ref, right_ref = refs[2 * nr + nl:2 * nr + nl + 2]
    outs = refs[2 * nr + nl + 2:-3]
    acc, sel, inter = refs[-3:]
    me = lax.axis_index("mpo")
    total = sums[0][...]
    for part in sums[1:]:
        total = total + part[...]
    scale = jnp.sqrt(jnp.sum(total, keepdims=True) / elements + 1e-06)
    values = [t[...] for t in tiles]
    if chip_pair:
        values = [jnp.where(me == 0, values[1 - i], values[i]) for i in range(2)]
    acc[...] = jnp.zeros_like(acc)
    for terms, value in zip(lists, values):
        vec = (value / scale).astype(jnp.bfloat16)
        picked = pick_entries(terms, sel)
        apply_list(terms, sel, picked, vec, left_ref, right_ref, acc, inter, dims)
    if nl == 4:
        own, keep, give = outs
        tile = own.shape[0]
        half = tile // 2
        own[...] = acc[0]
        keep[:tile] = acc[1 + me]
        keep[tile:] = acc[3, pl.ds(pl.multiple_of(half * me, half), half)]
        give[:tile] = acc[2 - me]
        give[tile:] = acc[3, pl.ds(pl.multiple_of(half - half * me, half), half)]
    else:
        for s in range(nl):
            outs[s][...] = acc[s]


def permute(value, target):
    nl, nr, nm = lax.axis_size("left"), lax.axis_size("right"), lax.axis_size("mpo")
    pairs = []
    for p in range(nl):
        for t in range(nr):
            for m in range(nm):
                to = target(p, t, m)
                pairs.append(((p * nr + t) * nm + m, (to[0] * nr + to[1]) * nm + to[2]))
    return lax.ppermute(value, ("left", "right", "mpo"), pairs)


def local(theta, left_env, right_env, terms):
    tile = theta.shape[-1]
    lt_dev = left_env.shape[1]
    rt_dev = right_env.shape[1]
    left_flat = left_env.reshape(-1, tile, tile)
    right_flat = right_env.reshape(-1, tile, tile)
    nl = lax.axis_size("left")
    nr = lax.axis_size("right")
    chip_pair = nr == 2
    rows, fields = terms.shape[-2:]
    entries = jnp.transpose(terms, (0, 1, 4, 2, 3)).reshape(fields, 1, rows)
    dims = (lt_dev, rt_dev, CAP * nr == rows)
    swap_cores = lambda x: permute(x, lambda p, t, m: (p, t, 1 - m))
    lists = [entries] + [permute(entries, lambda p, t, m, s=s: (p, t ^ s, m)) for s in range(1, nr)]
    thetas = [theta] + [permute(theta, lambda p, t, m, s=s: (p, t ^ s, 1 - m)) for s in range(1, nr)]
    stack = jax.ShapeDtypeStruct((nl, tile, tile), jnp.float32)
    scratch = [pltpu.SMEM((rows + 1,), jnp.int32), pltpu.VMEM((CAP, tile, tile), jnp.bfloat16)]
    params = pltpu.CompilerParams(vmem_limit_bytes=32 << 20)

    left_flat, right_flat = pl.pallas_call(
        load_kernel,
        out_shape=[jax.ShapeDtypeStruct(x.shape, x.dtype) for x in (left_flat, right_flat)],
        in_specs=[HBM] * 2,
        out_specs=[VMEM] * 2,
        scratch_shapes=[pltpu.SemaphoreType.DMA((2,))],
        compiler_params=pltpu.CompilerParams(vmem_limit_bytes=51 << 20),
        name="load",
    )(left_flat, right_flat)
    own_part = pl.pallas_call(
        functools.partial(own_kernel, dims),
        out_shape=stack,
        in_specs=[SMEM] + [VMEM] * 3,
        out_specs=VMEM,
        scratch_shapes=scratch,
        compiler_params=params,
        name="first_own",
    )(entries, theta, left_flat, right_flat)
    part = pl.pallas_call(
        functools.partial(rest_kernel, dims, nr - 1),
        out_shape=stack,
        in_specs=[SMEM] * (nr - 1) + [VMEM] * (nr + 2),
        out_specs=VMEM,
        scratch_shapes=scratch,
        compiler_params=params,
        name="first_rest",
    )(*lists[1:], *thetas[1:], left_flat, right_flat, own_part)

    chip = part + swap_cores(part)
    if chip_pair:
        mine = None
        for s in [*range(1, nl), 0]:
            got = permute(chip[s], lambda p, t, m: (p ^ s, t ^ m, 1 - m))
            mine = got if mine is None else mine + got
        other = swap_cores(mine)
        tiles = [mine, other]
        h_theta = jnp.where(lax.axis_index("mpo") == 1, mine, other)
    else:
        h_theta = chip[0]
        for s in range(1, nl):
            h_theta = h_theta + permute(chip[s], lambda p, t, m: (p ^ s, t, 1 - m))
        tiles = [h_theta]
        for s in range(1, nr):
            tiles.append(permute(h_theta, lambda p, t, m: (p, t ^ s, 1 - m)))
    squares = sum(jnp.sum((x * x).reshape(tile // 8, 8, tile), axis=0) for x in tiles)
    sums = [squares]
    for s in [2, 1, 3] if nl == 4 else range(1, nl):
        sums.append(permute(squares, lambda p, t, m: (p ^ s, t, 1 - m)))

    flat = lambda rows: jax.ShapeDtypeStruct((rows, tile), jnp.float32)
    out_shape = [flat(tile), flat(tile * 3 // 2), flat(tile * 3 // 2)] if nl == 4 else [flat(tile)] * nl
    parts = pl.pallas_call(
        functools.partial(second_kernel, dims, nr, nl, chip_pair, nl * nr * tile * tile),
        out_shape=out_shape,
        in_specs=[SMEM] * nr + [VMEM] * (nr + nl + 2),
        out_specs=[VMEM] * len(out_shape),
        scratch_shapes=[pltpu.VMEM((nl, tile, tile), jnp.float32)] + scratch,
        compiler_params=params,
        name="second_product",
    )(*lists, *tiles, *sums, left_flat, right_flat)
    half = parts[0]
    if nl == 4:
        _, keep, give = parts
        chip = keep + swap_cores(give)
        near = permute(chip[:tile], lambda p, t, m: (p ^ (1 + m), t, 1 - m))
        far = permute(chip[tile:], lambda p, t, m: (p ^ 3, t, 1 - m))
        first = lax.axis_index("mpo") == 1
        none = jnp.zeros_like(far)
        placed = jnp.concatenate([jnp.where(first, far, none), jnp.where(first, none, far)], axis=0)
        half = half + near + placed
    else:
        for s in range(1, nl):
            half = half + permute(parts[s], lambda p, t, m: (p ^ s, t, 1 - m))
    h_second = half + swap_cores(half)
    return h_theta[None], h_second[None]


def solution(mesh):
    in_specs = (
        P(("groups", "left", "right"), None, None),
        P(("groups", "mpo"), "left", None, None),
        P(("groups", "mpo"), "right", None, None),
        P(("groups", "left"), "right", "mpo", None, None),
    )
    out_specs = (
        P(("groups", "left", "right"), None, None),
        P(("groups", "left", "right"), None, None),
    )
    return jax.shard_map(local, mesh=mesh, in_specs=in_specs, out_specs=out_specs, check_vma=False)
```

```python
import functools

import jax
import jax.numpy as jnp
from jax import lax
from jax.experimental import pallas as pl
from jax.experimental.pallas import tpu as pltpu
from jax.sharding import PartitionSpec as P

CAP = 8
VMEM = pl.BlockSpec(memory_space=pltpu.VMEM)
HBM = pl.BlockSpec(memory_space=pltpu.HBM)
SMEM = pl.BlockSpec(memory_space=pltpu.SMEM)


def dot(a, b):
    return jnp.dot(a, b, preferred_element_type=jnp.float32)


def pick_entries(terms, sel):
    me_right = lax.axis_index("right")
    count = jnp.int32(0)
    for e in range(terms.shape[-1]):
        sel[count] = jnp.int32(e)
        count = count + (terms[1, 0, e] == me_right).astype(jnp.int32)
    return count


def apply_list(terms, sel, count, vec, left_ref, right_ref, acc, inter, dims):
    lt_dev, rt_dev, exact = dims
    me_left = lax.axis_index("left")
    fields, _, rows = terms.shape
    per = (fields - 2) // 2
    tile = vec.shape[-1]

    def spread(e, y):
        base = (terms[0, 0, e] // lt_dev) * rt_dev
        for j in range(per):
            product = dot(y, right_ref[base + terms[2 + j, 0, e]])
            acc[terms[2 + per + j, 0, e] ^ me_left] += product

    if exact:
        picks = jnp.concatenate([left_ref[terms[0, 0, sel[n]]] for n in range(CAP)], axis=0)
        inter[...] = dot(picks, vec).astype(jnp.bfloat16).reshape(CAP, tile, tile)
        for n in range(CAP):
            spread(sel[n], inter[n])
    else:

        def one(n):
            e = sel[n]
            spread(e, dot(left_ref[terms[0, 0, e]], vec).astype(jnp.bfloat16))

        pl.loop(0, count)(one)


def load_kernel(left_hbm, right_hbm, left_ref, right_ref, sems):
    copies = [
        pltpu.make_async_copy(left_hbm, left_ref, sems.at[0]),
        pltpu.make_async_copy(right_hbm, right_ref, sems.at[1]),
    ]
    for copy in copies:
        copy.start()
    for copy in copies:
        copy.wait()


def own_kernel(dims, terms, theta, left_ref, right_ref, out, sel, inter):
    out[...] = jnp.zeros_like(out)
    count = pick_entries(terms, sel)
    apply_list(terms, sel, count, theta[0], left_ref, right_ref, out, inter, dims)


def rest_kernel(dims, count, *refs):
    lists = refs[:count]
    thetas = refs[count:2 * count]
    left_ref, right_ref, start, out, sel, inter = refs[2 * count:]
    out[...] = start[...]
    for terms, theta in zip(lists, thetas):
        picked = pick_entries(terms, sel)
        apply_list(terms, sel, picked, theta[0], left_ref, right_ref, out, inter, dims)


def second_kernel(dims, nr, nl, chip_pair, elements, *refs):
    lists = refs[:nr]
    tiles = refs[nr:2 * nr]
    sums = refs[2 * nr:2 * nr + nl]
    left_ref, right_ref = refs[2 * nr + nl:2 * nr + nl + 2]
    outs = refs[2 * nr + nl + 2:-3]
    acc, sel, inter = refs[-3:]
    me = lax.axis_index("mpo")
    total = sums[0][...]
    for part in sums[1:]:
        total = total + part[...]
    scale = jnp.sqrt(jnp.sum(total, keepdims=True) / elements + 1e-06)
    values = [t[...] for t in tiles]
    if chip_pair:
        values = [jnp.where(me == 0, values[1 - i], values[i]) for i in range(2)]
    acc[...] = jnp.zeros_like(acc)
    for terms, value in zip(lists, values):
        vec = (value / scale).astype(jnp.bfloat16)
        picked = pick_entries(terms, sel)
        apply_list(terms, sel, picked, vec, left_ref, right_ref, acc, inter, dims)
    if nl == 4:
        own, keep, give = outs
        tile = own.shape[0]
        half = tile // 2
        own[...] = acc[0]
        keep[:tile] = acc[1 + me]
        keep[tile:] = acc[3, pl.ds(pl.multiple_of(half * me, half), half)]
        give[:tile] = acc[2 - me]
        give[tile:] = acc[3, pl.ds(pl.multiple_of(half - half * me, half), half)]
    else:
        for s in range(nl):
            outs[s][...] = acc[s]


def permute(value, target):
    nl, nr, nm = lax.axis_size("left"), lax.axis_size("right"), lax.axis_size("mpo")
    pairs = []
    for p in range(nl):
        for t in range(nr):
            for m in range(nm):
                to = target(p, t, m)
                pairs.append(((p * nr + t) * nm + m, (to[0] * nr + to[1]) * nm + to[2]))
    return lax.ppermute(value, ("left", "right", "mpo"), pairs)


def local(theta, left_env, right_env, terms):
    tile = theta.shape[-1]
    lt_dev = left_env.shape[1]
    rt_dev = right_env.shape[1]
    left_flat = left_env.reshape(-1, tile, tile)
    right_flat = right_env.reshape(-1, tile, tile)
    nl = lax.axis_size("left")
    nr = lax.axis_size("right")
    chip_pair = nr == 2
    rows, fields = terms.shape[-2:]
    entries = jnp.transpose(terms, (0, 1, 4, 2, 3)).reshape(fields, 1, rows)
    dims = (lt_dev, rt_dev, CAP * nr == rows)
    swap_cores = lambda x: permute(x, lambda p, t, m: (p, t, 1 - m))
    lists = [entries] + [permute(entries, lambda p, t, m, s=s: (p, t ^ s, m)) for s in range(1, nr)]
    thetas = [theta] + [permute(theta, lambda p, t, m, s=s: (p, t ^ s, 1 - m)) for s in range(1, nr)]
    stack = jax.ShapeDtypeStruct((nl, tile, tile), jnp.float32)
    scratch = [pltpu.SMEM((rows + 1,), jnp.int32), pltpu.VMEM((CAP, tile, tile), jnp.bfloat16)]
    params = pltpu.CompilerParams(vmem_limit_bytes=32 << 20)

    left_flat, right_flat = pl.pallas_call(
        load_kernel,
        out_shape=[jax.ShapeDtypeStruct(x.shape, x.dtype) for x in (left_flat, right_flat)],
        in_specs=[HBM] * 2,
        out_specs=[VMEM] * 2,
        scratch_shapes=[pltpu.SemaphoreType.DMA((2,))],
        compiler_params=pltpu.CompilerParams(vmem_limit_bytes=51 << 20),
        name="load",
    )(left_flat, right_flat)
    own_part = pl.pallas_call(
        functools.partial(own_kernel, dims),
        out_shape=stack,
        in_specs=[SMEM] + [VMEM] * 3,
        out_specs=VMEM,
        scratch_shapes=scratch,
        compiler_params=params,
        name="first_own",
    )(entries, theta, left_flat, right_flat)
    part = pl.pallas_call(
        functools.partial(rest_kernel, dims, nr - 1),
        out_shape=stack,
        in_specs=[SMEM] * (nr - 1) + [VMEM] * (nr + 2),
        out_specs=VMEM,
        scratch_shapes=scratch,
        compiler_params=params,
        name="first_rest",
    )(*lists[1:], *thetas[1:], left_flat, right_flat, own_part)

    chip = part + swap_cores(part)
    if chip_pair:
        mine = None
        for s in [3, 1, 2, 0] if nl == 4 else range(nl):
            got = permute(chip[s], lambda p, t, m: (p ^ s, t ^ m, 1 - m))
            mine = got if mine is None else mine + got
        other = swap_cores(mine)
        tiles = [mine, other]
        h_theta = jnp.where(lax.axis_index("mpo") == 1, mine, other)
    else:
        h_theta = chip[0]
        for s in range(1, nl):
            h_theta = h_theta + permute(chip[s], lambda p, t, m: (p ^ s, t, 1 - m))
        tiles = [h_theta]
        for s in range(1, nr):
            tiles.append(permute(h_theta, lambda p, t, m: (p, t ^ s, 1 - m)))
    squares = sum(jnp.sum((x * x).reshape(tile // 8, 8, tile), axis=0) for x in tiles)
    sums = [squares]
    for s in [2, 1, 3] if nl == 4 else range(1, nl):
        sums.append(permute(squares, lambda p, t, m: (p ^ s, t, 1 - m)))

    flat = lambda rows: jax.ShapeDtypeStruct((rows, tile), jnp.float32)
    out_shape = [flat(tile), flat(tile * 3 // 2), flat(tile * 3 // 2)] if nl == 4 else [flat(tile)] * nl
    parts = pl.pallas_call(
        functools.partial(second_kernel, dims, nr, nl, chip_pair, nl * nr * tile * tile),
        out_shape=out_shape,
        in_specs=[SMEM] * nr + [VMEM] * (nr + nl + 2),
        out_specs=[VMEM] * len(out_shape),
        scratch_shapes=[pltpu.VMEM((nl, tile, tile), jnp.float32)] + scratch,
        compiler_params=params,
        name="second_product",
    )(*lists, *tiles, *sums, left_flat, right_flat)
    half = parts[0]
    if nl == 4:
        _, keep, give = parts
        chip = keep + swap_cores(give)
        near = permute(chip[:tile], lambda p, t, m: (p ^ (1 + m), t, 1 - m))
        far = permute(chip[tile:], lambda p, t, m: (p ^ 3, t, 1 - m))
        first = lax.axis_index("mpo") == 1
        none = jnp.zeros_like(far)
        placed = jnp.concatenate([jnp.where(first, far, none), jnp.where(first, none, far)], axis=0)
        half = half + near + placed
    else:
        for s in range(1, nl):
            half = half + permute(parts[s], lambda p, t, m: (p ^ s, t, 1 - m))
    h_second = half + swap_cores(half)
    return h_theta[None], h_second[None]


def solution(mesh):
    in_specs = (
        P(("groups", "left", "right"), None, None),
        P(("groups", "mpo"), "left", None, None),
        P(("groups", "mpo"), "right", None, None),
        P(("groups", "left"), "right", "mpo", None, None),
    )
    out_specs = (
        P(("groups", "left", "right"), None, None),
        P(("groups", "left", "right"), None, None),
    )
    return jax.shard_map(local, mesh=mesh, in_specs=in_specs, out_specs=out_specs, check_vma=False)
```

```python
import functools

import jax
import jax.numpy as jnp
from jax import lax
from jax.experimental import pallas as pl
from jax.experimental.pallas import tpu as pltpu
from jax.sharding import PartitionSpec as P

BLOCKS = 4
CAP = 8
VMEM = pl.BlockSpec(memory_space=pltpu.VMEM)
HBM = pl.BlockSpec(memory_space=pltpu.HBM)


def dot(a, b):
    return jnp.dot(a, b, preferred_element_type=jnp.float32)


def pick_entries(terms, words, lt_dev, rt_dev):
    me_right = lax.axis_index("right")
    me_left = lax.axis_index("left")
    fields, _, rows = terms.shape
    per = (fields - 2) // 2
    bits = lambda count: (count - 1).bit_length()
    left_bits, target_bits = bits(2 * lt_dev), bits(lax.axis_size("right"))
    tile_bits, out_bits = bits(rt_dev), bits(lax.axis_size("left"))
    shift = left_bits + target_bits
    tiles = terms[0] + (terms[1] << left_bits)
    offsets = terms[2 + per] ^ me_left
    for j in range(per):
        tiles = tiles + (terms[2 + j] << (shift + j * tile_bits))
        if j:
            offsets = offsets + ((terms[2 + per + j] ^ me_left) << (j * out_bits))
    count = jnp.int32(0)
    for e in range(rows):
        word = tiles[0, e]
        words[0, count] = word
        words[1, count] = offsets[0, e]
        target = (word >> left_bits) & ((1 << target_bits) - 1)
        count = count + (target == me_right).astype(jnp.int32)

    def read(n):
        word, outs = words[0, n], words[1, n]
        left = word & ((1 << left_bits) - 1)
        base = (left // lt_dev) * rt_dev
        rights = [base + ((word >> (shift + j * tile_bits)) & ((1 << tile_bits) - 1)) for j in range(per)]
        return left, rights, [(outs >> (j * out_bits)) & ((1 << out_bits) - 1) for j in range(per)]

    return count, read


def blocks(accs):
    size = accs[0].shape[-2]
    return [(slice(i * size, (i + 1) * size), acc) for i, acc in enumerate(accs)]


def apply_list(picked, vec, left_ref, right_ref, accs, inter, exact):
    count, read = picked
    tile = vec.shape[-1]

    def spread(rights, outs, y):
        for right, out in zip(rights, outs):
            product = dot(y, right_ref[right])
            for rows, acc in blocks(accs):
                acc[out] += product[rows]

    if exact:
        entries = [read(n) for n in range(CAP)]
        picks = jnp.concatenate([left_ref[entry[0]] for entry in entries], axis=0)
        inter[...] = dot(picks, vec).astype(jnp.bfloat16).reshape(CAP, tile, tile)
        for n, (_, rights, outs) in enumerate(entries):
            spread(rights, outs, inter[n])
    else:

        def one(n):
            left, rights, outs = read(n)
            spread(rights, outs, dot(left_ref[left], vec).astype(jnp.bfloat16))

        pl.loop(0, count)(one)


def load_kernel(left_hbm, right_hbm, left_ref, right_ref, sems):
    copies = [
        pltpu.make_async_copy(left_hbm, left_ref, sems.at[0]),
        pltpu.make_async_copy(right_hbm, right_ref, sems.at[1]),
    ]
    for copy in copies:
        copy.start()
    for copy in copies:
        copy.wait()


def own_kernel(dims, terms, theta, left_ref, right_ref, *refs):
    *accs, words, inter = refs
    picked = pick_entries(terms, words.at[0], *dims[:2])
    for acc in accs:
        acc[...] = jnp.zeros_like(acc)
    apply_list(picked, theta[0], left_ref, right_ref, accs, inter.at[0], dims[2])


def rest_kernel(dims, count, *refs):
    lists = refs[:count]
    thetas = refs[count:2 * count]
    left_ref, right_ref = refs[2 * count:2 * count + 2]
    starts = refs[2 * count + 2:2 * count + 2 + BLOCKS]
    out, *accs, words, inter = refs[2 * count + 2 + BLOCKS:]
    picked = [pick_entries(terms, words.at[i], *dims[:2]) for i, terms in enumerate(lists)]
    for acc, start in zip(accs, starts):
        acc[...] = start[...]
    for i, theta in enumerate(thetas):
        apply_list(picked[i], theta[0], left_ref, right_ref, accs, inter.at[i], dims[2])
    for rows, acc in blocks(accs):
        out[:, rows] = acc[...]


def second_kernel(dims, nr, nl, chip_pair, elements, *refs):
    lists = refs[:nr]
    tiles = refs[nr:2 * nr]
    sums = refs[2 * nr:2 * nr + nl]
    left_ref, right_ref = refs[2 * nr + nl:2 * nr + nl + 2]
    outs = refs[2 * nr + nl + 2:-2 - BLOCKS]
    *accs, words, inter = refs[-2 - BLOCKS:]
    picked = [pick_entries(terms, words.at[i], *dims[:2]) for i, terms in enumerate(lists)]
    me = lax.axis_index("mpo")
    total = sums[0][...]
    for part in sums[1:]:
        total = total + part[...]
    scale = 1.0 / jnp.sqrt(jnp.sum(total, keepdims=True) / elements + 1e-06)
    values = [t[...] for t in tiles]
    if chip_pair:
        values = [jnp.where(me == 0, values[1 - i], values[i]) for i in range(2)]
    for acc in accs:
        acc[...] = jnp.zeros_like(acc)
    for i, value in enumerate(values):
        vec = (value * scale).astype(jnp.bfloat16)
        apply_list(picked[i], vec, left_ref, right_ref, accs, inter.at[i], dims[2])
    if nl == 4:
        own, keep, give = outs
        tile = own.shape[0]
        for rows, acc in blocks(accs):
            own[rows] = acc[0]
            keep[rows] = acc[1 + me]
            give[rows] = acc[2 - me]
        half = len(accs) // 2
        for (rows, low), (_, high) in zip(blocks(accs[:half]), blocks(accs[half:])):
            rows = slice(tile + rows.start, tile + rows.stop)
            keep[rows] = jnp.where(me == 0, low[3], high[3])
            give[rows] = jnp.where(me == 0, high[3], low[3])
    else:
        for s in range(nl):
            for rows, acc in blocks(accs):
                outs[s][rows] = acc[s]


def permute(value, target):
    nl, nr, nm = lax.axis_size("left"), lax.axis_size("right"), lax.axis_size("mpo")
    pairs = []
    for p in range(nl):
        for t in range(nr):
            for m in range(nm):
                to = target(p, t, m)
                pairs.append(((p * nr + t) * nm + m, (to[0] * nr + to[1]) * nm + to[2]))
    return lax.ppermute(value, ("left", "right", "mpo"), pairs)


def local(theta, left_env, right_env, terms):
    tile = theta.shape[-1]
    lt_dev = left_env.shape[1]
    rt_dev = right_env.shape[1]
    left_flat = left_env.reshape(-1, tile, tile)
    right_flat = right_env.reshape(-1, tile, tile)
    nl = lax.axis_size("left")
    nr = lax.axis_size("right")
    chip_pair = nr == 2
    rows, fields = terms.shape[-2:]
    entries = jnp.transpose(terms, (0, 1, 4, 2, 3)).reshape(fields, 1, rows)
    dims = (lt_dev, rt_dev, CAP * nr == rows)
    swap_cores = lambda x: permute(x, lambda p, t, m: (p, t, 1 - m))
    lists = [entries] + [permute(entries, lambda p, t, m, s=s: (p, t ^ s, m)) for s in range(1, nr)]
    thetas = [theta] + [permute(theta, lambda p, t, m, s=s: (p, t ^ s, 1 - m)) for s in range(1, nr)]
    stack = jax.ShapeDtypeStruct((nl, tile, tile), jnp.float32)
    part_shapes = [((nl, tile // BLOCKS, tile), jnp.float32)] * BLOCKS
    accs = [pltpu.VMEM(*shape) for shape in part_shapes]
    scratch = [pltpu.SMEM((nr, 2, rows + 1), jnp.int32), pltpu.VMEM((nr, CAP, tile, tile), jnp.bfloat16)]
    params = pltpu.CompilerParams(vmem_limit_bytes=32 << 20)

    left_flat, right_flat = pl.pallas_call(
        load_kernel,
        out_shape=[jax.ShapeDtypeStruct(x.shape, x.dtype) for x in (left_flat, right_flat)],
        in_specs=[HBM] * 2,
        out_specs=[VMEM] * 2,
        scratch_shapes=[pltpu.SemaphoreType.DMA((2,))],
        compiler_params=pltpu.CompilerParams(vmem_limit_bytes=51 << 20),
        name="load",
    )(left_flat, right_flat)
    own_parts = pl.pallas_call(
        functools.partial(own_kernel, dims),
        out_shape=[jax.ShapeDtypeStruct(*shape) for shape in part_shapes],
        in_specs=[VMEM] * 4,
        out_specs=[VMEM] * BLOCKS,
        scratch_shapes=scratch,
        compiler_params=params,
        name="first_own",
    )(entries, theta, left_flat, right_flat)
    part = pl.pallas_call(
        functools.partial(rest_kernel, dims, nr - 1),
        out_shape=stack,
        in_specs=[VMEM] * (2 * nr + BLOCKS),
        out_specs=VMEM,
        scratch_shapes=accs + scratch,
        compiler_params=params,
        name="first_rest",
    )(*lists[1:], *thetas[1:], left_flat, right_flat, *own_parts)

    chip = part + swap_cores(part)
    if chip_pair:
        mine = None
        for s in [3, 1, 2, 0] if nl == 4 else range(nl):
            got = permute(chip[s], lambda p, t, m: (p ^ s, t ^ m, 1 - m))
            mine = got if mine is None else mine + got
        other = swap_cores(mine)
        tiles = [mine, other]
        h_theta = jnp.where(lax.axis_index("mpo") == 1, mine, other)
    else:
        h_theta = chip[0]
        for s in range(1, nl):
            h_theta = h_theta + permute(chip[s], lambda p, t, m: (p ^ s, t, 1 - m))
        tiles = [h_theta]
        for s in range(1, nr):
            tiles.append(permute(h_theta, lambda p, t, m: (p, t ^ s, 1 - m)))
    squares = sum(jnp.sum((x * x).reshape(tile // 8, 8, tile), axis=0) for x in tiles)
    sums = [squares]
    for s in [2, 1, 3] if nl == 4 else range(1, nl):
        sums.append(permute(squares, lambda p, t, m: (p ^ s, t, 1 - m)))

    flat = lambda rows: jax.ShapeDtypeStruct((rows, tile), jnp.float32)
    out_shape = [flat(tile), flat(tile * 3 // 2), flat(tile * 3 // 2)] if nl == 4 else [flat(tile)] * nl
    parts = pl.pallas_call(
        functools.partial(second_kernel, dims, nr, nl, chip_pair, nl * nr * tile * tile),
        out_shape=out_shape,
        in_specs=[VMEM] * (2 * nr + nl + 2),
        out_specs=[VMEM] * len(out_shape),
        scratch_shapes=accs + scratch,
        compiler_params=params,
        name="second_product",
    )(*lists, *tiles, *sums, left_flat, right_flat)
    half = parts[0]
    if nl == 4:
        _, keep, give = parts
        chip = keep + swap_cores(give)
        near = permute(chip[:tile], lambda p, t, m: (p ^ (1 + m), t, 1 - m))
        far = permute(chip[tile:], lambda p, t, m: (p ^ 3, t, 1 - m))
        first = lax.axis_index("mpo") == 1
        none = jnp.zeros_like(far)
        placed = jnp.concatenate([jnp.where(first, far, none), jnp.where(first, none, far)], axis=0)
        half = half + near + placed
    else:
        for s in range(1, nl):
            half = half + permute(parts[s], lambda p, t, m: (p ^ s, t, 1 - m))
    h_second = half + swap_cores(half)
    return h_theta[None], h_second[None]


def solution(mesh):
    in_specs = (
        P(("groups", "left", "right"), None, None),
        P(("groups", "mpo"), "left", None, None),
        P(("groups", "mpo"), "right", None, None),
        P(("groups", "left"), "right", "mpo", None, None),
    )
    out_specs = (
        P(("groups", "left", "right"), None, None),
        P(("groups", "left", "right"), None, None),
    )
    return jax.shard_map(local, mesh=mesh, in_specs=in_specs, out_specs=out_specs, check_vma=False)
```

```python
import functools

import jax
import jax.numpy as jnp
from jax import lax
from jax.experimental import pallas as pl
from jax.experimental.pallas import tpu as pltpu
from jax.sharding import PartitionSpec as P

BLOCKS = 4
CAP = 8
VMEM = pl.BlockSpec(memory_space=pltpu.VMEM)
HBM = pl.BlockSpec(memory_space=pltpu.HBM)


def dot(a, b):
    return jnp.dot(a, b, preferred_element_type=jnp.float32)


def pick_entries(terms, words, lt_dev, rt_dev):
    me_right = lax.axis_index("right")
    me_left = lax.axis_index("left")
    fields, _, rows = terms.shape
    per = (fields - 2) // 2
    bits = lambda count: (count - 1).bit_length()
    left_bits, target_bits = bits(2 * lt_dev), bits(lax.axis_size("right"))
    tile_bits, out_bits = bits(rt_dev), bits(lax.axis_size("left"))
    shift = left_bits + target_bits
    tiles = terms[0] + (terms[1] << left_bits)
    offsets = terms[2 + per] ^ me_left
    for j in range(per):
        tiles = tiles + (terms[2 + j] << (shift + j * tile_bits))
        if j:
            offsets = offsets + ((terms[2 + per + j] ^ me_left) << (j * out_bits))
    count = jnp.int32(0)
    for e in range(rows):
        word = tiles[0, e]
        words[0, count] = word
        words[1, count] = offsets[0, e]
        target = (word >> left_bits) & ((1 << target_bits) - 1)
        count = count + (target == me_right).astype(jnp.int32)

    def read(n):
        word, outs = words[0, n], words[1, n]
        left = word & ((1 << left_bits) - 1)
        base = (left // lt_dev) * rt_dev
        rights = [base + ((word >> (shift + j * tile_bits)) & ((1 << tile_bits) - 1)) for j in range(per)]
        return left, rights, [(outs >> (j * out_bits)) & ((1 << out_bits) - 1) for j in range(per)]

    return count, read


def blocks(accs):
    size = accs[0].shape[-2]
    return [(slice(i * size, (i + 1) * size), acc) for i, acc in enumerate(accs)]


def apply_list(picked, vec, left_ref, right_ref, accs, inter, exact):
    count, read = picked
    tile = vec.shape[-1]

    def spread(rights, outs, y):
        for right, out in zip(rights, outs):
            product = dot(y, right_ref[right])
            for rows, acc in blocks(accs):
                acc[out] += product[rows]

    if exact:
        entries = [read(n) for n in range(CAP)]
        picks = jnp.concatenate([left_ref[entry[0]] for entry in entries], axis=0)
        inter[...] = dot(picks, vec).astype(jnp.bfloat16).reshape(CAP, tile, tile)
        for n, (_, rights, outs) in enumerate(entries):
            spread(rights, outs, inter[n])
    else:

        def one(n):
            left, rights, outs = read(n)
            spread(rights, outs, dot(left_ref[left], vec).astype(jnp.bfloat16))

        pl.loop(0, count)(one)


def load_kernel(left_hbm, right_hbm, left_ref, right_ref, sems):
    copies = [
        pltpu.make_async_copy(left_hbm, left_ref, sems.at[0]),
        pltpu.make_async_copy(right_hbm, right_ref, sems.at[1]),
    ]
    for copy in copies:
        copy.start()
    for copy in copies:
        copy.wait()


def fold_squares(value):
    return jnp.sum((value * value).reshape(-1, 8, value.shape[-1]), axis=0)


def emit(accs, outs):
    if accs[0].shape[0] == 4:
        me = lax.axis_index("mpo")
        own, keep, give = outs
        tile = own.shape[0]
        for rows, acc in blocks(accs):
            own[rows] = acc[0]
            keep[rows] = acc[1 + me]
            give[rows] = acc[2 - me]
        half = len(accs) // 2
        for (rows, low), (_, high) in zip(blocks(accs[:half]), blocks(accs[half:])):
            rows = slice(tile + rows.start, tile + rows.stop)
            keep[rows] = jnp.where(me == 0, low[3], high[3])
            give[rows] = jnp.where(me == 0, high[3], low[3])
    else:
        for s, out in enumerate(outs):
            for rows, acc in blocks(accs):
                out[rows] = acc[s]


def own_kernel(dims, terms, theta, left_ref, right_ref, *refs):
    *accs, words, inter = refs
    picked = pick_entries(terms, words.at[0], *dims[:2])
    for acc in accs:
        acc[...] = jnp.zeros_like(acc)
    apply_list(picked, theta[0], left_ref, right_ref, accs, inter.at[0], dims[2])


def rest_kernel(dims, count, *refs):
    lists = refs[:count]
    thetas = refs[count:2 * count]
    left_ref, right_ref = refs[2 * count:2 * count + 2]
    starts = refs[2 * count + 2:2 * count + 2 + BLOCKS]
    outs = refs[2 * count + 2 + BLOCKS:-2 - BLOCKS]
    *accs, words, inter = refs[-2 - BLOCKS:]
    picked = [pick_entries(terms, words.at[i], *dims[:2]) for i, terms in enumerate(lists)]
    for acc, start in zip(accs, starts):
        acc[...] = start[...]
    for i, theta in enumerate(thetas):
        apply_list(picked[i], theta[0], left_ref, right_ref, accs, inter.at[i], dims[2])
    emit(accs, outs)


def second_kernel(dims, nr, count, elements, *refs):
    lists = refs[:nr]
    tiles = refs[nr:2 * nr]
    sums = refs[2 * nr:2 * nr + count]
    left_ref, right_ref = refs[2 * nr + count:2 * nr + count + 2]
    outs = refs[2 * nr + count + 2:-2 - BLOCKS]
    *accs, words, inter = refs[-2 - BLOCKS:]
    picked = [pick_entries(terms, words.at[i], *dims[:2]) for i, terms in enumerate(lists)]
    values = [t[...] for t in tiles]
    total = sum(fold_squares(value) for value in values[1:])
    for part in sums:
        total = total + part[...]
    scale = 1.0 / jnp.sqrt(jnp.sum(total, keepdims=True) / elements + 1e-06)
    for acc in accs:
        acc[...] = jnp.zeros_like(acc)
    for i, value in enumerate(values):
        vec = (value * scale).astype(jnp.bfloat16)
        apply_list(picked[i], vec, left_ref, right_ref, accs, inter.at[i], dims[2])
    emit(accs, outs)


def permute(value, target):
    nl, nr, nm = lax.axis_size("left"), lax.axis_size("right"), lax.axis_size("mpo")
    pairs = []
    for p in range(nl):
        for t in range(nr):
            for m in range(nm):
                to = target(p, t, m)
                pairs.append(((p * nr + t) * nm + m, (to[0] * nr + to[1]) * nm + to[2]))
    return lax.ppermute(value, ("left", "right", "mpo"), pairs)


def local(theta, left_env, right_env, terms):
    tile = theta.shape[-1]
    lt_dev = left_env.shape[1]
    rt_dev = right_env.shape[1]
    left_flat = left_env.reshape(-1, tile, tile)
    right_flat = right_env.reshape(-1, tile, tile)
    nl = lax.axis_size("left")
    nr = lax.axis_size("right")
    rows, fields = terms.shape[-2:]
    entries = jnp.transpose(terms, (0, 1, 4, 2, 3)).reshape(fields, 1, rows)
    dims = (lt_dev, rt_dev, CAP * nr == rows)
    swap_cores = lambda x: permute(x, lambda p, t, m: (p, t, 1 - m))
    lists = [entries] + [permute(entries, lambda p, t, m, s=s: (p, t ^ s, m)) for s in range(1, nr)]
    thetas = [theta] + [permute(theta, lambda p, t, m, s=s: (p, t ^ s, 1 - m)) for s in range(1, nr)]
    part_shapes = [((nl, tile // BLOCKS, tile), jnp.float32)] * BLOCKS
    accs = [pltpu.VMEM(*shape) for shape in part_shapes]
    scratch = [pltpu.SMEM((nr, 2, rows + 1), jnp.int32), pltpu.VMEM((nr, CAP, tile, tile), jnp.bfloat16)]
    params = pltpu.CompilerParams(vmem_limit_bytes=32 << 20)

    def reduce_tiles(parts):
        half = parts[0]
        if nl == 4:
            _, keep, give = parts
            chip = keep + swap_cores(give)
            near = permute(chip[:tile], lambda p, t, m: (p ^ (1 + m), t, 1 - m))
            far = permute(chip[tile:], lambda p, t, m: (p ^ 3, t, 1 - m))
            first = lax.axis_index("mpo") == 1
            none = jnp.zeros_like(far)
            placed = jnp.concatenate([jnp.where(first, far, none), jnp.where(first, none, far)], axis=0)
            half = half + near + placed
        else:
            for s in range(1, nl):
                half = half + permute(parts[s], lambda p, t, m: (p ^ s, t, 1 - m))
        return half

    left_flat, right_flat = pl.pallas_call(
        load_kernel,
        out_shape=[jax.ShapeDtypeStruct(x.shape, x.dtype) for x in (left_flat, right_flat)],
        in_specs=[HBM] * 2,
        out_specs=[VMEM] * 2,
        scratch_shapes=[pltpu.SemaphoreType.DMA((2,))],
        compiler_params=pltpu.CompilerParams(vmem_limit_bytes=51 << 20),
        name="load",
    )(left_flat, right_flat)
    own_parts = pl.pallas_call(
        functools.partial(own_kernel, dims),
        out_shape=[jax.ShapeDtypeStruct(*shape) for shape in part_shapes],
        in_specs=[VMEM] * 4,
        out_specs=[VMEM] * BLOCKS,
        scratch_shapes=scratch,
        compiler_params=params,
        name="first_own",
    )(entries, theta, left_flat, right_flat)
    flat = lambda rows: jax.ShapeDtypeStruct((rows, tile), jnp.float32)
    out_shape = [flat(tile), flat(tile * 3 // 2), flat(tile * 3 // 2)] if nl == 4 else [flat(tile)] * nl
    parts = pl.pallas_call(
        functools.partial(rest_kernel, dims, nr - 1),
        out_shape=out_shape,
        in_specs=[VMEM] * (2 * nr + BLOCKS),
        out_specs=[VMEM] * len(out_shape),
        scratch_shapes=accs + scratch,
        compiler_params=params,
        name="first_rest",
    )(*lists[1:], *thetas[1:], left_flat, right_flat, *own_parts)

    half = reduce_tiles(parts)
    halves = [permute(half, lambda p, t, m: (p, t ^ s, m)) for s in range(1, nr)]
    h_theta = half + swap_cores(half)
    neighbours = [x + swap_cores(x) for x in halves]
    squares = fold_squares(h_theta)
    if nr == 2:
        sums = [permute(squares, lambda p, t, m: (p ^ s, t ^ m, m)) for s in range(1, nl)]
        others = sum(sums[1:], sums[0])
        sums = [squares, others, swap_cores(others)]
    else:
        row = squares + sum(fold_squares(x) for x in neighbours)
        sums = [squares] + [permute(row, lambda p, t, m: (p ^ s, t, 1 - m)) for s in range(1, nl)]
    tiles = [h_theta] + neighbours

    parts = pl.pallas_call(
        functools.partial(second_kernel, dims, nr, len(sums), nl * nr * tile * tile),
        out_shape=out_shape,
        in_specs=[VMEM] * (2 * nr + len(sums) + 2),
        out_specs=[VMEM] * len(out_shape),
        scratch_shapes=accs + scratch,
        compiler_params=params,
        name="second_product",
    )(*lists, *tiles, *sums, left_flat, right_flat)
    half = reduce_tiles(parts)
    h_second = half + swap_cores(half)
    return h_theta[None], h_second[None]


def solution(mesh):
    in_specs = (
        P(("groups", "left", "right"), None, None),
        P(("groups", "mpo"), "left", None, None),
        P(("groups", "mpo"), "right", None, None),
        P(("groups", "left"), "right", "mpo", None, None),
    )
    out_specs = (
        P(("groups", "left", "right"), None, None),
        P(("groups", "left", "right"), None, None),
    )
    return jax.shard_map(local, mesh=mesh, in_specs=in_specs, out_specs=out_specs, check_vma=False)
```

```python
import functools

import jax
import jax.numpy as jnp
from jax import lax
from jax.experimental import pallas as pl
from jax.experimental.pallas import tpu as pltpu
from jax.sharding import PartitionSpec as P

BLOCKS = 4
CAP = 8
VMEM = pl.BlockSpec(memory_space=pltpu.VMEM)
HBM = pl.BlockSpec(memory_space=pltpu.HBM)


def dot(a, b):
    return jnp.dot(a, b, preferred_element_type=jnp.float32)


def pick_entries(terms, words, lt_dev, rt_dev):
    me_right = lax.axis_index("right")
    me_left = lax.axis_index("left")
    fields, _, rows = terms.shape
    per = (fields - 2) // 2
    bits = lambda count: (count - 1).bit_length()
    left_bits, target_bits = bits(2 * lt_dev), bits(lax.axis_size("right"))
    tile_bits, out_bits = bits(rt_dev), bits(lax.axis_size("left"))
    shift = left_bits + target_bits
    tiles = terms[0] + (terms[1] << left_bits)
    offsets = terms[2 + per] ^ me_left
    for j in range(per):
        tiles = tiles + (terms[2 + j] << (shift + j * tile_bits))
        if j:
            offsets = offsets + ((terms[2 + per + j] ^ me_left) << (j * out_bits))
    count = jnp.int32(0)
    for e in range(rows):
        word = tiles[0, e]
        words[0, count] = word
        words[1, count] = offsets[0, e]
        target = (word >> left_bits) & ((1 << target_bits) - 1)
        count = count + (target == me_right).astype(jnp.int32)

    def read(n):
        word, outs = words[0, n], words[1, n]
        left = word & ((1 << left_bits) - 1)
        base = (left // lt_dev) * rt_dev
        rights = [base + ((word >> (shift + j * tile_bits)) & ((1 << tile_bits) - 1)) for j in range(per)]
        return left, rights, [(outs >> (j * out_bits)) & ((1 << out_bits) - 1) for j in range(per)]

    return count, read


def blocks(accs):
    size = accs[0].shape[-2]
    return [(slice(i * size, (i + 1) * size), acc) for i, acc in enumerate(accs)]


def apply_list(picked, vec, left_ref, right_ref, accs, inter, exact):
    count, read = picked
    tile = vec.shape[-1]

    def spread(rights, outs, y):
        for right, out in zip(rights, outs):
            product = dot(y, right_ref[right])
            for rows, acc in blocks(accs):
                acc[out] += product[rows]

    if exact:
        entries = [read(n) for n in range(CAP)]
        picks = jnp.concatenate([left_ref[entry[0]] for entry in entries], axis=0)
        inter[...] = dot(picks, vec).astype(jnp.bfloat16).reshape(CAP, tile, tile)
        for n, (_, rights, outs) in enumerate(entries):
            spread(rights, outs, inter[n])
    else:

        def one(n):
            left, rights, outs = read(n)
            spread(rights, outs, dot(left_ref[left], vec).astype(jnp.bfloat16))

        pl.loop(0, count)(one)


def load_kernel(left_hbm, right_hbm, left_ref, right_ref, sems):
    copies = [
        pltpu.make_async_copy(left_hbm, left_ref, sems.at[0]),
        pltpu.make_async_copy(right_hbm, right_ref, sems.at[1]),
    ]
    for copy in copies:
        copy.start()
    for copy in copies:
        copy.wait()


def fold_squares(value):
    return jnp.sum((value * value).reshape(-1, 8, value.shape[-1]), axis=0)


def emit(accs, outs):
    me = lax.axis_index("mpo")
    offsets = range(len(outs))
    if accs[0].shape[0] == 4:
        offsets = (0, 2 - me, 1 + me, 3)
    for s, out in zip(offsets, outs):
        for rows, acc in blocks(accs):
            out[rows] = acc[s]


def own_kernel(dims, terms, theta, left_ref, right_ref, *refs):
    *accs, words, inter = refs
    picked = pick_entries(terms, words.at[0], *dims[:2])
    for acc in accs:
        acc[...] = jnp.zeros_like(acc)
    apply_list(picked, theta[0], left_ref, right_ref, accs, inter.at[0], dims[2])


def rest_kernel(dims, count, *refs):
    lists = refs[:count]
    thetas = refs[count:2 * count]
    left_ref, right_ref = refs[2 * count:2 * count + 2]
    starts = refs[2 * count + 2:2 * count + 2 + BLOCKS]
    outs = refs[2 * count + 2 + BLOCKS:-2 - BLOCKS]
    *accs, words, inter = refs[-2 - BLOCKS:]
    picked = [pick_entries(terms, words.at[i], *dims[:2]) for i, terms in enumerate(lists)]
    for acc, start in zip(accs, starts):
        acc[...] = start[...]
    for i, theta in enumerate(thetas):
        apply_list(picked[i], theta[0], left_ref, right_ref, accs, inter.at[i], dims[2])
    emit(accs, outs)


def second_kernel(dims, nr, count, elements, *refs):
    lists = refs[:nr]
    tiles = refs[nr:2 * nr]
    sums = refs[2 * nr:2 * nr + count]
    left_ref, right_ref = refs[2 * nr + count:2 * nr + count + 2]
    outs = refs[2 * nr + count + 2:-2 - BLOCKS]
    *accs, words, inter = refs[-2 - BLOCKS:]
    picked = [pick_entries(terms, words.at[i], *dims[:2]) for i, terms in enumerate(lists)]
    values = [t[...] for t in tiles]
    total = sum(fold_squares(value) for value in values[1:])
    for part in sums:
        total = total + part[...]
    scale = 1.0 / jnp.sqrt(jnp.sum(total, keepdims=True) / elements + 1e-06)
    for acc in accs:
        acc[...] = jnp.zeros_like(acc)
    for i, value in enumerate(values):
        vec = (value * scale).astype(jnp.bfloat16)
        apply_list(picked[i], vec, left_ref, right_ref, accs, inter.at[i], dims[2])
    emit(accs, outs)


def permute(value, target):
    nl, nr, nm = lax.axis_size("left"), lax.axis_size("right"), lax.axis_size("mpo")
    pairs = []
    for p in range(nl):
        for t in range(nr):
            for m in range(nm):
                to = target(p, t, m)
                pairs.append(((p * nr + t) * nm + m, (to[0] * nr + to[1]) * nm + to[2]))
    return lax.ppermute(value, ("left", "right", "mpo"), pairs)


def local(theta, left_env, right_env, terms):
    tile = theta.shape[-1]
    lt_dev = left_env.shape[1]
    rt_dev = right_env.shape[1]
    left_flat = left_env.reshape(-1, tile, tile)
    right_flat = right_env.reshape(-1, tile, tile)
    nl = lax.axis_size("left")
    nr = lax.axis_size("right")
    rows, fields = terms.shape[-2:]
    entries = jnp.transpose(terms, (0, 1, 4, 2, 3)).reshape(fields, 1, rows)
    dims = (lt_dev, rt_dev, CAP * nr == rows)
    swap_cores = lambda x: permute(x, lambda p, t, m: (p, t, 1 - m))
    lists = [entries] + [permute(entries, lambda p, t, m, s=s: (p, t ^ s, m)) for s in range(1, nr)]
    thetas = [theta] + [permute(theta, lambda p, t, m, s=s: (p, t ^ s, 1 - m)) for s in range(1, nr)]
    part_shapes = [((nl, tile // BLOCKS, tile), jnp.float32)] * BLOCKS
    accs = [pltpu.VMEM(*shape) for shape in part_shapes]
    scratch = [pltpu.SMEM((nr, 2, rows + 1), jnp.int32), pltpu.VMEM((nr, CAP, tile, tile), jnp.bfloat16)]
    params = pltpu.CompilerParams(vmem_limit_bytes=32 << 20)

    def reduce_tiles(parts):
        half = parts[0]
        if nl == 4:
            _, keep, give, far = parts
            far = permute(far, lambda p, t, m: (p ^ 3, t, 1 - m))
            near = permute(keep + swap_cores(give), lambda p, t, m: (p ^ (2 - m), t, 1 - m))
            half = half + near + far
        else:
            for s in range(1, nl):
                half = half + permute(parts[s], lambda p, t, m: (p ^ s, t, 1 - m))
        return half

    left_flat, right_flat = pl.pallas_call(
        load_kernel,
        out_shape=[jax.ShapeDtypeStruct(x.shape, x.dtype) for x in (left_flat, right_flat)],
        in_specs=[HBM] * 2,
        out_specs=[VMEM] * 2,
        scratch_shapes=[pltpu.SemaphoreType.DMA((2,))],
        compiler_params=pltpu.CompilerParams(vmem_limit_bytes=51 << 20),
        name="load",
    )(left_flat, right_flat)
    own_parts = pl.pallas_call(
        functools.partial(own_kernel, dims),
        out_shape=[jax.ShapeDtypeStruct(*shape) for shape in part_shapes],
        in_specs=[VMEM] * 4,
        out_specs=[VMEM] * BLOCKS,
        scratch_shapes=scratch,
        compiler_params=params,
        name="first_own",
    )(entries, theta, left_flat, right_flat)
    out_shape = [jax.ShapeDtypeStruct((tile, tile), jnp.float32)] * nl
    parts = pl.pallas_call(
        functools.partial(rest_kernel, dims, nr - 1),
        out_shape=out_shape,
        in_specs=[VMEM] * (2 * nr + BLOCKS),
        out_specs=[VMEM] * len(out_shape),
        scratch_shapes=accs + scratch,
        compiler_params=params,
        name="first_rest",
    )(*lists[1:], *thetas[1:], left_flat, right_flat, *own_parts)

    half = reduce_tiles(parts)
    halves = [permute(half, lambda p, t, m: (p, t ^ s, m)) for s in range(1, nr)]
    h_theta = half + swap_cores(half)
    neighbours = [x + swap_cores(x) for x in halves]
    squares = fold_squares(h_theta)
    if nr == 2:
        sums = [permute(squares, lambda p, t, m: (p ^ s, t ^ m, m)) for s in range(1, nl)]
        others = sum(sums[1:], sums[0])
        sums = [squares, others, swap_cores(others)]
    else:
        row = squares + sum(fold_squares(x) for x in neighbours)
        sums = [squares] + [permute(row, lambda p, t, m: (p ^ s, t, 1 - m)) for s in range(1, nl)]
    tiles = [h_theta] + neighbours

    parts = pl.pallas_call(
        functools.partial(second_kernel, dims, nr, len(sums), nl * nr * tile * tile),
        out_shape=out_shape,
        in_specs=[VMEM] * (2 * nr + len(sums) + 2),
        out_specs=[VMEM] * len(out_shape),
        scratch_shapes=accs + scratch,
        compiler_params=params,
        name="second_product",
    )(*lists, *tiles, *sums, left_flat, right_flat)
    half = reduce_tiles(parts)
    h_second = half + swap_cores(half)
    return h_theta[None], h_second[None]


def solution(mesh):
    in_specs = (
        P(("groups", "left", "right"), None, None),
        P(("groups", "mpo"), "left", None, None),
        P(("groups", "mpo"), "right", None, None),
        P(("groups", "left"), "right", "mpo", None, None),
    )
    out_specs = (
        P(("groups", "left", "right"), None, None),
        P(("groups", "left", "right"), None, None),
    )
    return jax.shard_map(local, mesh=mesh, in_specs=in_specs, out_specs=out_specs, check_vma=False)
```

```python
import functools

import jax
import jax.numpy as jnp
from jax import lax
from jax.experimental import pallas as pl
from jax.experimental.pallas import tpu as pltpu
from jax.sharding import PartitionSpec as P

BLOCKS = 4
CAP = 8
VMEM = pl.BlockSpec(memory_space=pltpu.VMEM)
HBM = pl.BlockSpec(memory_space=pltpu.HBM)


def dot(a, b):
    return jnp.dot(a, b, preferred_element_type=jnp.float32)


def reader(words, per, lt_dev, rt_dev):
    bits = lambda count: (count - 1).bit_length()
    left_bits, tile_bits, out_bits = bits(2 * lt_dev), bits(rt_dev), bits(lax.axis_size("left"))
    shift = left_bits + bits(lax.axis_size("right"))

    def read(n):
        word, outs = words(0, n), words(1, n)
        left = word & ((1 << left_bits) - 1)
        base = (left // lt_dev) * rt_dev
        rights = [base + ((word >> (shift + j * tile_bits)) & ((1 << tile_bits) - 1)) for j in range(per)]
        return left, rights, [(outs >> (j * out_bits)) & ((1 << out_bits) - 1) for j in range(per)]

    return read


def pick_entries(terms, words, lt_dev, rt_dev):
    me_right = lax.axis_index("right")
    me_left = lax.axis_index("left")
    fields, _, rows = terms.shape
    per = (fields - 2) // 2
    bits = lambda count: (count - 1).bit_length()
    left_bits, target_bits = bits(2 * lt_dev), bits(lax.axis_size("right"))
    tile_bits, out_bits = bits(rt_dev), bits(lax.axis_size("left"))
    shift = left_bits + target_bits
    tiles = terms[0] + (terms[1] << left_bits)
    offsets = terms[2 + per] ^ me_left
    for j in range(per):
        tiles = tiles + (terms[2 + j] << (shift + j * tile_bits))
        if j:
            offsets = offsets + ((terms[2 + per + j] ^ me_left) << (j * out_bits))
    count = jnp.int32(0)
    for e in range(rows):
        word = tiles[0, e]
        words[0, count] = word
        words[1, count] = offsets[0, e]
        target = (word >> left_bits) & ((1 << target_bits) - 1)
        count = count + (target == me_right).astype(jnp.int32)

    read = reader(lambda row, n: words[row, n], per, lt_dev, rt_dev)
    return count, read


def blocks(accs):
    size = accs[0].shape[-2]
    return [(slice(i * size, (i + 1) * size), acc) for i, acc in enumerate(accs)]


def apply_list(picked, vec, left_ref, right_ref, accs, inter, exact):
    count, read = picked
    tile = vec.shape[-1]

    def spread(rights, outs, y):
        for right, out in zip(rights, outs):
            product = dot(y, right_ref[right])
            for rows, acc in blocks(accs):
                acc[out] += product[rows]

    if exact:
        entries = [read(n) for n in range(CAP)]
        picks = jnp.concatenate([left_ref[entry[0]] for entry in entries], axis=0)
        inter[...] = dot(picks, vec).astype(jnp.bfloat16).reshape(CAP, tile, tile)
        for n, (_, rights, outs) in enumerate(entries):
            spread(rights, outs, inter[n])
    else:

        def one(n):
            left, rights, outs = read(n)
            spread(rights, outs, dot(left_ref[left], vec).astype(jnp.bfloat16))

        pl.loop(0, count)(one)


def write_plan(words, out):
    lane = lax.broadcasted_iota(jnp.int32, (1, out.shape[1]), 1)
    for k in range(2):
        row = jnp.zeros((1, out.shape[1]), jnp.int32)
        for n in range(CAP):
            row = jnp.where(lane == n, words[k, n], row)
        out[k:k + 1] = row


def picked_of(key, words, dims):
    if not dims[2]:
        return pick_entries(key, words, *dims[:2])
    rows = [key[k:k + 1] for k in range(2)]
    return CAP, reader(lambda row, n: rows[row][0, n], dims[3], *dims[:2])


def load_kernel(left_hbm, right_hbm, left_ref, right_ref, sems):
    copies = [
        pltpu.make_async_copy(left_hbm, left_ref, sems.at[0]),
        pltpu.make_async_copy(right_hbm, right_ref, sems.at[1]),
    ]
    for copy in copies:
        copy.start()
    for copy in copies:
        copy.wait()


def fold_squares(value):
    return jnp.sum((value * value).reshape(-1, 8, value.shape[-1]), axis=0)


def emit(accs, outs):
    me = lax.axis_index("mpo")
    offsets = range(len(outs))
    if accs[0].shape[0] == 4:
        offsets = (0, 2 - me, 1 + me, 3)
    for s, out in zip(offsets, outs):
        for rows, acc in blocks(accs):
            out[rows] = acc[s]


def own_kernel(dims, terms, theta, left_ref, right_ref, *refs):
    *accs, plan, words, inter = refs
    picked = pick_entries(terms, words.at[0], *dims[:2])
    write_plan(words.at[0], plan)
    for acc in accs:
        acc[...] = jnp.zeros_like(acc)
    apply_list(picked, theta[0], left_ref, right_ref, accs, inter.at[0], dims[2])


def rest_kernel(dims, count, *refs):
    lists = refs[:count]
    thetas = refs[count:2 * count]
    left_ref, right_ref = refs[2 * count:2 * count + 2]
    starts = refs[2 * count + 2:2 * count + 2 + BLOCKS]
    *outs, plans = refs[2 * count + 2 + BLOCKS:-2 - BLOCKS]
    *accs, words, inter = refs[-2 - BLOCKS:]
    picked = [pick_entries(terms, words.at[i], *dims[:2]) for i, terms in enumerate(lists)]
    for i in range(count):
        write_plan(words.at[i], plans.at[i])
    for acc, start in zip(accs, starts):
        acc[...] = start[...]
    for i, theta in enumerate(thetas):
        apply_list(picked[i], theta[0], left_ref, right_ref, accs, inter.at[i], dims[2])
    emit(accs, outs)


def second_kernel(dims, nr, count, elements, *refs):
    keys = refs[:nr]
    tiles = refs[nr:2 * nr]
    sums = refs[2 * nr:2 * nr + count]
    left_ref, right_ref = refs[2 * nr + count:2 * nr + count + 2]
    outs = refs[2 * nr + count + 2:-2 - BLOCKS]
    *accs, words, inter = refs[-2 - BLOCKS:]
    picked = [picked_of(key, words.at[i], dims) for i, key in enumerate(keys)]
    values = [t[...] for t in tiles]
    total = sums[0][...]
    for part in sums[1:]:
        total = total + part[...]
    scale = 1.0 / jnp.sqrt(jnp.sum(total, keepdims=True) / elements + 1e-06)
    for acc in accs:
        acc[...] = jnp.zeros_like(acc)
    for i, value in enumerate(values):
        vec = (value * scale).astype(jnp.bfloat16)
        apply_list(picked[i], vec, left_ref, right_ref, accs, inter.at[i], dims[2])
    emit(accs, outs)


def permute(value, target):
    nl, nr, nm = lax.axis_size("left"), lax.axis_size("right"), lax.axis_size("mpo")
    pairs = []
    for p in range(nl):
        for t in range(nr):
            for m in range(nm):
                to = target(p, t, m)
                pairs.append(((p * nr + t) * nm + m, (to[0] * nr + to[1]) * nm + to[2]))
    return lax.ppermute(value, ("left", "right", "mpo"), pairs)


def local(theta, left_env, right_env, terms):
    tile = theta.shape[-1]
    lt_dev = left_env.shape[1]
    rt_dev = right_env.shape[1]
    left_flat = left_env.reshape(-1, tile, tile)
    right_flat = right_env.reshape(-1, tile, tile)
    nl = lax.axis_size("left")
    nr = lax.axis_size("right")
    rows, fields = terms.shape[-2:]
    entries = jnp.transpose(terms, (0, 1, 4, 2, 3)).reshape(fields, 1, rows)
    dims = (lt_dev, rt_dev, CAP * nr == rows, (fields - 2) // 2)
    swap_cores = lambda x: permute(x, lambda p, t, m: (p, t, 1 - m))
    lists = [entries] + [permute(entries, lambda p, t, m, s=s: (p, t ^ s, m)) for s in range(1, nr)]
    thetas = [theta] + [permute(theta, lambda p, t, m, s=s: (p, t ^ s, 1 - m)) for s in range(1, nr)]
    part_shapes = [((nl, tile // BLOCKS, tile), jnp.float32)] * BLOCKS
    accs = [pltpu.VMEM(*shape) for shape in part_shapes]
    scratch = [pltpu.SMEM((nr, 2, rows + 1), jnp.int32), pltpu.VMEM((nr, CAP, tile, tile), jnp.bfloat16)]
    params = pltpu.CompilerParams(vmem_limit_bytes=32 << 20)

    def reduce_tiles(parts):
        half = parts[0]
        if nl == 4:
            _, keep, give, far = parts
            far = permute(far, lambda p, t, m: (p ^ 3, t, 1 - m))
            near = permute(keep + swap_cores(give), lambda p, t, m: (p ^ (2 - m), t, 1 - m))
            half = half + near + far
        else:
            for s in range(1, nl):
                half = half + permute(parts[s], lambda p, t, m: (p ^ s, t, 1 - m))
        return half

    left_flat, right_flat = pl.pallas_call(
        load_kernel,
        out_shape=[jax.ShapeDtypeStruct(x.shape, x.dtype) for x in (left_flat, right_flat)],
        in_specs=[HBM] * 2,
        out_specs=[VMEM] * 2,
        scratch_shapes=[pltpu.SemaphoreType.DMA((2,))],
        compiler_params=pltpu.CompilerParams(vmem_limit_bytes=51 << 20),
        name="load",
    )(left_flat, right_flat)
    plan_shape = jax.ShapeDtypeStruct((2, tile), jnp.int32)
    *own_parts, own_plan = pl.pallas_call(
        functools.partial(own_kernel, dims),
        out_shape=[jax.ShapeDtypeStruct(*shape) for shape in part_shapes] + [plan_shape],
        in_specs=[VMEM] * 4,
        out_specs=[VMEM] * (BLOCKS + 1),
        scratch_shapes=scratch,
        compiler_params=params,
        name="first_own",
    )(entries, theta, left_flat, right_flat)
    out_shape = [jax.ShapeDtypeStruct((tile, tile), jnp.float32)] * nl
    *parts, plans = pl.pallas_call(
        functools.partial(rest_kernel, dims, nr - 1),
        out_shape=out_shape + [jax.ShapeDtypeStruct((nr - 1, 2, tile), jnp.int32)],
        in_specs=[VMEM] * (2 * nr + BLOCKS),
        out_specs=[VMEM] * (nl + 1),
        scratch_shapes=accs + scratch,
        compiler_params=params,
        name="first_rest",
    )(*lists[1:], *thetas[1:], left_flat, right_flat, *own_parts)
    keys = [own_plan, *plans] if dims[2] else lists

    half = reduce_tiles(parts)
    halves = [permute(half, lambda p, t, m: (p, t ^ s, m)) for s in range(1, nr)]
    h_theta = half + swap_cores(half)
    neighbours = [x + swap_cores(x) for x in halves]
    squares = fold_squares(h_theta)
    if nr == 2:
        sums = [permute(squares, lambda p, t, m: (p ^ s, t ^ m, m)) for s in range(1, nl)]
        others = sum(sums[1:], sums[0])
        sums = [squares + fold_squares(neighbours[0]), others, swap_cores(others)]
    else:
        row = squares + sum(fold_squares(x) for x in neighbours)
        sums = [row] + [permute(row, lambda p, t, m: (p ^ s, t, 1 - m)) for s in range(1, nl)]
    tiles = [h_theta] + neighbours

    parts = pl.pallas_call(
        functools.partial(second_kernel, dims, nr, len(sums), nl * nr * tile * tile),
        out_shape=out_shape,
        in_specs=[VMEM] * (2 * nr + len(sums) + 2),
        out_specs=[VMEM] * len(out_shape),
        scratch_shapes=accs + scratch,
        compiler_params=params,
        name="second_product",
    )(*keys, *tiles, *sums, left_flat, right_flat)
    half = reduce_tiles(parts)
    h_second = half + swap_cores(half)
    return h_theta[None], h_second[None]


def solution(mesh):
    in_specs = (
        P(("groups", "left", "right"), None, None),
        P(("groups", "mpo"), "left", None, None),
        P(("groups", "mpo"), "right", None, None),
        P(("groups", "left"), "right", "mpo", None, None),
    )
    out_specs = (
        P(("groups", "left", "right"), None, None),
        P(("groups", "left", "right"), None, None),
    )
    return jax.shard_map(local, mesh=mesh, in_specs=in_specs, out_specs=out_specs, check_vma=False)
```

```python
import functools

import jax
import jax.numpy as jnp
from jax import lax
from jax.experimental import pallas as pl
from jax.experimental.pallas import tpu as pltpu
from jax.sharding import PartitionSpec as P

BLOCKS = 4
CAP = 8
VMEM = pl.BlockSpec(memory_space=pltpu.VMEM)
HBM = pl.BlockSpec(memory_space=pltpu.HBM)


def dot(a, b):
    return jnp.dot(a, b, preferred_element_type=jnp.float32)


def reader(words, per, lt_dev, rt_dev):
    bits = lambda count: (count - 1).bit_length()
    left_bits, tile_bits, out_bits = bits(2 * lt_dev), bits(rt_dev), bits(lax.axis_size("left"))
    shift = left_bits + bits(lax.axis_size("right"))

    def read(n):
        word, outs = words(0, n), words(1, n)
        left = word & ((1 << left_bits) - 1)
        base = (left // lt_dev) * rt_dev
        rights = [base + ((word >> (shift + j * tile_bits)) & ((1 << tile_bits) - 1)) for j in range(per)]
        return left, rights, [(outs >> (j * out_bits)) & ((1 << out_bits) - 1) for j in range(per)]

    return read


def pick_entries(terms, words, lt_dev, rt_dev):
    me_right = lax.axis_index("right")
    me_left = lax.axis_index("left")
    fields, _, rows = terms.shape
    per = (fields - 2) // 2
    bits = lambda count: (count - 1).bit_length()
    left_bits, target_bits = bits(2 * lt_dev), bits(lax.axis_size("right"))
    tile_bits, out_bits = bits(rt_dev), bits(lax.axis_size("left"))
    shift = left_bits + target_bits
    tiles = terms[0] + (terms[1] << left_bits)
    offsets = terms[2 + per] ^ me_left
    for j in range(per):
        tiles = tiles + (terms[2 + j] << (shift + j * tile_bits))
        if j:
            offsets = offsets + ((terms[2 + per + j] ^ me_left) << (j * out_bits))
    count = jnp.int32(0)
    for e in range(rows):
        word = tiles[0, e]
        words[0, count] = word
        words[1, count] = offsets[0, e]
        target = (word >> left_bits) & ((1 << target_bits) - 1)
        count = count + (target == me_right).astype(jnp.int32)

    read = reader(lambda row, n: words[row, n], per, lt_dev, rt_dev)
    return count, read


def blocks(accs):
    size = accs[0].shape[-2]
    return [(slice(i * size, (i + 1) * size), acc) for i, acc in enumerate(accs)]


def apply_list(picked, vec, left_ref, right_ref, accs, inter, exact):
    count, read = picked
    tile = vec.shape[-1]

    def spread(rights, outs, y):
        for right, out in zip(rights, outs):
            product = dot(y, right_ref[right])
            for rows, acc in blocks(accs):
                acc[out] += product[rows]

    if exact:
        entries = [read(n) for n in range(CAP)]
        picks = jnp.concatenate([left_ref[entry[0]] for entry in entries], axis=0)
        inter[...] = dot(picks, vec).astype(jnp.bfloat16).reshape(CAP, tile, tile)
        for n, (_, rights, outs) in enumerate(entries):
            spread(rights, outs, inter[n])
    else:

        def one(n):
            left, rights, outs = read(n)
            spread(rights, outs, dot(left_ref[left], vec).astype(jnp.bfloat16))

        pl.loop(0, count)(one)


def write_plan(words, out):
    lane = lax.broadcasted_iota(jnp.int32, (1, out.shape[1]), 1)
    for k in range(2):
        row = jnp.zeros((1, out.shape[1]), jnp.int32)
        for n in range(CAP):
            row = jnp.where(lane == n, words[k, n], row)
        out[k:k + 1] = row


def picked_of(key, words, dims):
    if not dims[2]:
        return pick_entries(key, words, *dims[:2])
    rows = [key[k:k + 1] for k in range(2)]
    return CAP, reader(lambda row, n: rows[row][0, n], dims[3], *dims[:2])


def load_kernel(left_hbm, right_hbm, left_ref, right_ref, sems):
    copies = [
        pltpu.make_async_copy(left_hbm, left_ref, sems.at[0]),
        pltpu.make_async_copy(right_hbm, right_ref, sems.at[1]),
    ]
    for copy in copies:
        copy.start()
    for copy in copies:
        copy.wait()


def fold_squares(value):
    return jnp.sum((value * value).reshape(-1, 8, value.shape[-1]), axis=0)


def emit(accs, outs):
    me = lax.axis_index("mpo")
    offsets = range(len(outs))
    if accs[0].shape[0] == 4:
        offsets = (0, 2 - me, 1 + me, 3)
    for s, out in zip(offsets, outs):
        for rows, acc in blocks(accs):
            out[rows] = acc[s]


def own_kernel(dims, terms, theta, left_ref, right_ref, *refs):
    *accs, plan, words, inter = refs
    picked = pick_entries(terms, words.at[0], *dims[:2])
    write_plan(words.at[0], plan)
    for acc in accs:
        acc[...] = jnp.zeros_like(acc)
    apply_list(picked, theta[0], left_ref, right_ref, accs, inter.at[0], dims[2])


def rest_kernel(dims, count, *refs):
    lists = refs[:count]
    thetas = refs[count:2 * count]
    left_ref, right_ref = refs[2 * count:2 * count + 2]
    starts = refs[2 * count + 2:2 * count + 2 + BLOCKS]
    *outs, plans = refs[2 * count + 2 + BLOCKS:-2 - BLOCKS]
    *accs, words, inter = refs[-2 - BLOCKS:]
    picked = [pick_entries(terms, words.at[i], *dims[:2]) for i, terms in enumerate(lists)]
    for i in range(count):
        write_plan(words.at[i], plans.at[i])
    for acc, start in zip(accs, starts):
        acc[...] = start[...]
    for i, theta in enumerate(thetas):
        apply_list(picked[i], theta[0], left_ref, right_ref, accs, inter.at[i], dims[2])
    emit(accs, outs)


def second_kernel(dims, nr, count, elements, *refs):
    keys = refs[:nr]
    tiles = refs[nr:2 * nr]
    sums = refs[2 * nr:2 * nr + count]
    left_ref, right_ref = refs[2 * nr + count:2 * nr + count + 2]
    outs = refs[2 * nr + count + 2:-2 - BLOCKS]
    *accs, words, inter = refs[-2 - BLOCKS:]
    picked = [picked_of(key, words.at[i], dims) for i, key in enumerate(keys)]
    values = [t[...] for t in tiles]
    total = sums[0][...]
    for part in sums[1:]:
        total = total + part[...]
    scale = 1.0 / jnp.sqrt(jnp.sum(total, keepdims=True) / elements + 1e-06)
    for acc in accs:
        acc[...] = jnp.zeros_like(acc)
    for i, value in enumerate(values):
        vec = (value * scale).astype(jnp.bfloat16)
        apply_list(picked[i], vec, left_ref, right_ref, accs, inter.at[i], dims[2])
    emit(accs, outs)


def permute(value, target):
    nl, nr, nm = lax.axis_size("left"), lax.axis_size("right"), lax.axis_size("mpo")
    pairs = []
    for p in range(nl):
        for t in range(nr):
            for m in range(nm):
                to = target(p, t, m)
                pairs.append(((p * nr + t) * nm + m, (to[0] * nr + to[1]) * nm + to[2]))
    return lax.ppermute(value, ("left", "right", "mpo"), pairs)


def local(theta, left_env, right_env, terms):
    tile = theta.shape[-1]
    lt_dev = left_env.shape[1]
    rt_dev = right_env.shape[1]
    left_flat = left_env.reshape(-1, tile, tile)
    right_flat = right_env.reshape(-1, tile, tile)
    nl = lax.axis_size("left")
    nr = lax.axis_size("right")
    rows, fields = terms.shape[-2:]
    entries = jnp.transpose(terms, (0, 1, 4, 2, 3)).reshape(fields, 1, rows)
    dims = (lt_dev, rt_dev, CAP * nr == rows, (fields - 2) // 2)
    swap_cores = lambda x: permute(x, lambda p, t, m: (p, t, 1 - m))
    lists = [entries] + [permute(entries, lambda p, t, m, s=s: (p, t ^ s, m)) for s in range(1, nr)]
    thetas = [theta] + [permute(theta, lambda p, t, m, s=s: (p, t ^ s, 1 - m)) for s in range(1, nr)]
    part_shapes = [((nl, tile // BLOCKS, tile), jnp.float32)] * BLOCKS
    accs = [pltpu.VMEM(*shape) for shape in part_shapes]
    scratch = [pltpu.SMEM((nr, 2, rows + 1), jnp.int32), pltpu.VMEM((nr, CAP, tile, tile), jnp.bfloat16)]
    params = pltpu.CompilerParams(vmem_limit_bytes=32 << 20)

    def reduce_tiles(parts):
        half = parts[0]
        if nl == 4:
            _, keep, give, far = parts
            far = permute(far, lambda p, t, m: (p ^ 3, t, 1 - m))
            near = permute(keep + swap_cores(give), lambda p, t, m: (p ^ (2 - m), t, 1 - m))
            half = half + near + far
        else:
            for s in range(1, nl):
                half = half + permute(parts[s], lambda p, t, m: (p ^ s, t, 1 - m))
        return half

    left_flat, right_flat = pl.pallas_call(
        load_kernel,
        out_shape=[jax.ShapeDtypeStruct(x.shape, x.dtype) for x in (left_flat, right_flat)],
        in_specs=[HBM] * 2,
        out_specs=[VMEM] * 2,
        scratch_shapes=[pltpu.SemaphoreType.DMA((2,))],
        compiler_params=pltpu.CompilerParams(vmem_limit_bytes=51 << 20),
        name="load",
    )(left_flat, right_flat)
    plan_shape = jax.ShapeDtypeStruct((2, tile), jnp.int32)
    *own_parts, own_plan = pl.pallas_call(
        functools.partial(own_kernel, dims),
        out_shape=[jax.ShapeDtypeStruct(*shape) for shape in part_shapes] + [plan_shape],
        in_specs=[VMEM] * 4,
        out_specs=[VMEM] * (BLOCKS + 1),
        scratch_shapes=scratch,
        compiler_params=params,
        name="first_own",
    )(entries, theta, left_flat, right_flat)
    out_shape = [jax.ShapeDtypeStruct((tile, tile), jnp.float32)] * nl
    *parts, plans = pl.pallas_call(
        functools.partial(rest_kernel, dims, nr - 1),
        out_shape=out_shape + [jax.ShapeDtypeStruct((nr - 1, 2, tile), jnp.int32)],
        in_specs=[VMEM] * (2 * nr + BLOCKS),
        out_specs=[VMEM] * (nl + 1),
        scratch_shapes=accs + scratch,
        compiler_params=params,
        name="first_rest",
    )(*lists[1:], *thetas[1:], left_flat, right_flat, *own_parts)
    keys = [own_plan, *plans] if dims[2] else lists

    half = reduce_tiles(parts)
    halves = [permute(half, lambda p, t, m: (p, t ^ s, 1 - m)) for s in range(1, nr)]
    h_theta = half + swap_cores(half)
    neighbours = [x + swap_cores(x) for x in halves]
    squares = fold_squares(h_theta)
    if nr == 2:
        sums = [permute(squares, lambda p, t, m: (p ^ s, t ^ m, m)) for s in range(1, nl)]
        others = sum(sums[1:], sums[0])
        sums = [squares + fold_squares(neighbours[0]), others, swap_cores(others)]
    else:
        row = squares + sum(fold_squares(x) for x in neighbours)
        sums = [row] + [permute(row, lambda p, t, m: (p ^ s, t, 1 - m)) for s in range(1, nl)]
    tiles = [h_theta] + neighbours

    parts = pl.pallas_call(
        functools.partial(second_kernel, dims, nr, len(sums), nl * nr * tile * tile),
        out_shape=out_shape,
        in_specs=[VMEM] * (2 * nr + len(sums) + 2),
        out_specs=[VMEM] * len(out_shape),
        scratch_shapes=accs + scratch,
        compiler_params=params,
        name="second_product",
    )(*keys, *tiles, *sums, left_flat, right_flat)
    half = reduce_tiles(parts)
    h_second = half + swap_cores(half)
    return h_theta[None], h_second[None]


def solution(mesh):
    in_specs = (
        P(("groups", "left", "right"), None, None),
        P(("groups", "mpo"), "left", None, None),
        P(("groups", "mpo"), "right", None, None),
        P(("groups", "left"), "right", "mpo", None, None),
    )
    out_specs = (
        P(("groups", "left", "right"), None, None),
        P(("groups", "left", "right"), None, None),
    )
    return jax.shard_map(local, mesh=mesh, in_specs=in_specs, out_specs=out_specs, check_vma=False)
```
